256 devices in a mesh: depth: 8 (over y, core), cols: 32 (over z, x).
Axes of the slice: x: 4, y: 4, z: 8, core: 2. Of those that a mesh axis runs over, the one named last changes fastest.
Arguments:
- density: bfloat16 [1024, 4096, 128], P('depth', 'cols'), may hold values from -6 to 6
- occupancy: int32 [64, 256, 4], P('depth', 'cols'), may hold values from 0 to 1, as said below
- light_dir: float32 [3], replicated, may hold values from -4 to 4
- palette: float32 [4, 2], replicated, may hold values from 0.5 to 2
Outputs:
- final_image: float32 [4, 4096, 128], P(None, None, 'depth')
The draws below stay inside these ranges and needn't reach their ends.
Inputs may be any that keep to these rules, and one draw needn't show every extreme that they name: `occupancy`: 1 marks an occupied block of 16 x 16 x 32 cells; the share of occupied blocks differs from one depth layer of blocks to another.
All inputs are finite; a program needn't handle non-finite values.
Results may differ from the reference program's by a relative error of at most 0.0003.
Values may be sent and summed in bfloat16 or wider, within the bound.
No kernel may reach another device: no remote copies, remote signals or barrier semaphores. Data moves between devices by JAX's collectives and lax.ppermute only.
A program may use at most 192 MiB of HBM per device.

```python
import jax
import jax.numpy as jnp
from jax import lax

NY = 128
BLK_Z = 16
BLK_X = 16
BLK_Y = 32
NZ = 1024
NX = 4096
N_COLS = 32


def draw_occupancy(key, part):
    key = jax.random.fold_in(key, 11)
    layer_key, cell_key = jax.random.split(key)
    levels = jax.random.randint(layer_key, (NZ // BLK_Z, 1, 1), 1, 10)
    cells = jax.random.randint(cell_key, (NZ // BLK_Z, NX // BLK_X, NY // BLK_Y), 0, 10)
    return jnp.where(cells < levels, 1, 0).astype(jnp.int32)


def block_scale(own_key, shape, cuts, least, high):
    level = 1.0
    for position, blocks in cuts:
        steps = jax.random.uniform(jax.random.fold_in(jax.random.fold_in(own_key, 6), position), (blocks,), jnp.float32, least / len(cuts), high / len(cuts))
        level = level * jnp.repeat(jnp.exp(steps), shape[position] // blocks).reshape((-1,) + (1,) * (len(shape) - 1 - position))
    return level


def noise(key, shape, spread, bound, cuts=(), held_as=jnp.bfloat16):
    result = spread * jax.random.normal(key, shape, jnp.float32)
    if cuts:
        result = result * block_scale(key, shape, cuts, -0.22, 0.18)
    return jnp.clip(result, -bound, bound).astype(held_as)


def setup_inputs(seed: int = 0) -> dict:
    splits = jax.random.split(jax.random.key(seed), 5)
    density = noise(splits[0], (NZ, NX, NY), 1.0, 6.0, ((0, 8), (1, 32)))
    occupancy = draw_occupancy(jax.random.fold_in(splits[4], 71), 0)
    light_dir = noise(splits[2], (3,), 1.0, 4.0, (), jnp.float32)
    palette = jnp.clip(jax.random.uniform(splits[3], (4, 2), jnp.float32, 0.5, 2.0), 0.5, 2.0)
    return {"density": density, "occupancy": occupancy, "light_dir": light_dir, "palette": palette}


def expand_cells(values, occ):
    mz, mx, my = occ.shape
    planes, columns, rows = values.shape
    shaped = values.reshape(mz, planes // mz, mx, columns // mx, my, rows // my)
    return (shaped * occ.astype(jnp.float32)[:, None, :, None, :, None]).reshape(planes, columns, rows)

def render_block(values, occ, light_dir, palette, depth_total):
    centre = values[1:-1, 1:-1, 1:-1]
    grad_z = 0.5 * (values[2:, 1:-1, 1:-1] - values[:-2, 1:-1, 1:-1])
    grad_x = 0.5 * (values[1:-1, 2:, 1:-1] - values[1:-1, :-2, 1:-1])
    grad_y = 0.5 * (values[1:-1, 1:-1, 2:] - values[1:-1, 1:-1, :-2])
    factor = 1.0 / jnp.sqrt(1.0 + grad_z * grad_z + grad_x * grad_x + grad_y * grad_y)
    facing = (grad_z * light_dir[0] + grad_x * light_dir[1] + grad_y * light_dir[2]) * factor
    shading = 0.3 + 0.7 * jnp.tanh(jnp.abs(facing))
    optical = 3.0 / depth_total * jax.nn.softplus(palette[3, 0] * centre + palette[3, 1])
    optical = expand_cells(optical, occ)
    total = lax.optimization_barrier(jnp.sum(optical, axis=0))
    running = jnp.cumsum(optical, axis=0)
    ahead = total[None] - running
    weight = (1.0 - jnp.exp(-optical)) * jnp.exp(-ahead) * shading
    channels = [lax.optimization_barrier(jnp.sum(jax.nn.sigmoid(palette[c, 0] * centre + palette[c, 1]) * weight, axis=0)) for c in range(3)]
    channels.append(1.0 - jnp.exp(-total))
    return jnp.stack(channels, axis=0)

def reference(density, occupancy, light_dir, palette):
    depth_total, columns_total, rows_total = density.shape
    padded = jnp.pad(density, ((1, 1), (1, 1), (1, 1)))
    block_cols = columns_total // N_COLS
    occ_cols = block_cols // BLK_X

    def one_block(start):
        block = lax.dynamic_slice(padded, (jnp.int32(0), start, jnp.int32(0)), (depth_total + 2, block_cols + 2, rows_total + 2))
        occ = lax.dynamic_slice(occupancy, (jnp.int32(0), (start // block_cols * occ_cols).astype(jnp.int32), jnp.int32(0)), (occupancy.shape[0], occ_cols, occupancy.shape[2]))
        return render_block(block.astype(jnp.float32), occ, light_dir, palette, depth_total)
    starts = (jnp.arange(N_COLS, dtype=jnp.int32) * block_cols).astype(jnp.int32)
    blocks = lax.map(one_block, starts)
    return jnp.transpose(blocks, (1, 0, 2, 3)).reshape(4, columns_total, rows_total)
```

```python
import functools

import jax
import jax.numpy as jnp
import numpy as np
from jax import lax
from jax.experimental import pallas as pl
from jax.experimental.pallas import tpu as pltpu
from jax.sharding import PartitionSpec as P

BX = 16
LOG2E = 1.4426950408889634


def shift_matrix(n):
    m = np.zeros((n, n), np.float32)
    for j in range(n):
        if j + 1 < n:
            m[j + 1, j] = 1.0
        if j >= 1:
            m[j - 1, j] = -1.0
    return jnp.asarray(m, jnp.bfloat16)


def render_kernel(light, pal, here, left, right, zlow, zhigh, xlow, xhigh, occ, diff,
                  out, field, rows_grad, image, edge):
    step = pl.program_id(0)
    last = pl.num_programs(0) - 1
    planes, _, rows = here.shape
    f32 = jnp.float32

    field[pl.ds(1, planes), 8:8 + BX, :] = here[...].astype(f32)
    field[pl.ds(1, planes), 0:8, :] = left[:, 8:16, :].astype(f32)
    field[pl.ds(1, planes), 8 + BX:16 + BX, :] = right[:, 0:8, :].astype(f32)
    field[0, 8:8 + BX, :] = zlow[...].astype(f32)
    field[planes + 1, 8:8 + BX, :] = zhigh[...].astype(f32)

    @pl.when(step == 0)
    def _():
        edge[...] = xlow[...].astype(f32)

        @pl.loop(0, planes)
        def _(z):
            field[z + 1, 0:8, :] = jnp.broadcast_to(edge[pl.ds(z, 1), :], (8, rows))

    @pl.when(step == last)
    def _():
        edge[...] = xhigh[...].astype(f32)

        @pl.loop(0, planes)
        def _(z):
            field[z + 1, 8 + BX:16 + BX, :] = jnp.broadcast_to(edge[pl.ds(z, 1), :], (8, rows))

    rows_grad[...] = jnp.dot(
        here[...].reshape(planes * BX, rows), diff[...], preferred_element_type=f32
    ).reshape(planes, BX, rows)

    l0, l1, l2 = light[0], light[1], light[2]
    half = [(0.5 * pal[c, 0], 0.5 * pal[c, 1]) for c in range(3)]
    ext0, ext1 = pal[3, 0] * LOG2E, pal[3, 1] * LOG2E
    group = 16

    def body(k, carry):
        total, through, red, green, blue, white = carry
        zb = planes // group - 1 - k
        scale = jnp.broadcast_to(occ[zb, pl.ds(step, 1), :], (BX, rows))
        base = zb * group
        for zi in range(group - 1, -1, -1):
            z = base + zi
            v = field[z + 1, 8:8 + BX, :]
            gz = field[z + 2, 8:8 + BX, :] - field[z, 8:8 + BX, :]
            gx = field[z + 1, 9:9 + BX, :] - field[z + 1, 7:7 + BX, :]
            gy = rows_grad[z]
            norm = lax.rsqrt((gz * gz + gx * gx) + (gy * gy + 4.0))
            facing = jnp.abs((gz * l0 + gx * l1 + gy * l2) * norm)
            shade = 0.3 + 0.7 * jnp.tanh(facing)
            total = total + scale * jnp.log2(1.0 + jnp.exp2(v * ext0 + ext1))
            beyond = jnp.exp2(total)
            weight = (through - beyond) * shade
            through = beyond
            red = red + weight * jnp.tanh(v * half[0][0] + half[0][1])
            green = green + weight * jnp.tanh(v * half[1][0] + half[1][1])
            blue = blue + weight * jnp.tanh(v * half[2][0] + half[2][1])
            white = white + weight
        return total, through, red, green, blue, white

    zero = jnp.zeros((BX, rows), f32)
    total, _, red, green, blue, white = lax.fori_loop(
        0, planes // group, body, (zero, zero + 1.0, zero, zero, zero, zero)
    )
    at = pl.ds(pl.multiple_of(step * BX, BX), BX)
    image[0, at, :] = 0.5 * (white + red)
    image[1, at, :] = 0.5 * (white + green)
    image[2, at, :] = 0.5 * (white + blue)
    image[3, at, :] = total

    @pl.when(step == last)
    def _():
        slabs, _, block, _ = out.shape
        for c in range(4):
            turned = image[c].T
            for d in range(slabs):
                out[d, c] = turned[d * block:(d + 1) * block, :]


def render(density, occupancy, light_dir, palette, zlow, zhigh, xlow, xhigh, slabs):
    planes, columns, rows = density.shape
    steps = columns // BX
    full = lambda *shape: pl.BlockSpec(shape, lambda i: (0,) * len(shape))
    block = lambda move: pl.BlockSpec((planes, BX, rows), lambda i: (0, move(i), 0))
    return pl.pallas_call(
        render_kernel,
        grid=(steps,),
        in_specs=[
            pl.BlockSpec(memory_space=pltpu.SMEM),
            pl.BlockSpec(memory_space=pltpu.SMEM),
            block(lambda i: i),
            block(lambda i: jnp.maximum(i - 1, 0)),
            block(lambda i: jnp.minimum(i + 1, steps - 1)),
            pl.BlockSpec((BX, rows), lambda i: (i, 0)),
            pl.BlockSpec((BX, rows), lambda i: (i, 0)),
            full(planes, rows),
            full(planes, rows),
            full(*occupancy.shape),
            full(rows, rows),
        ],
        out_specs=full(slabs, 4, rows // slabs, columns),
        out_shape=jax.ShapeDtypeStruct((slabs, 4, rows // slabs, columns), jnp.float32),
        scratch_shapes=[
            pltpu.VMEM((planes + 2, BX + 16, rows), jnp.float32),
            pltpu.VMEM((planes, BX, rows), jnp.float32),
            pltpu.VMEM((4, columns, rows), jnp.float32),
            pltpu.VMEM((planes, rows), jnp.float32),
        ],
        compiler_params=pltpu.CompilerParams(vmem_limit_bytes=48 * 1024 * 1024),
    )(light_dir, palette, density, density, density, zlow, zhigh, xlow, xhigh, occupancy,
      shift_matrix(rows))


def composite_kernel(parts, out):
    slabs = parts.shape[0]
    total = parts[slabs - 1, 3]
    colours = [parts[slabs - 1, c] for c in range(3)]
    for d in range(slabs - 2, -1, -1):
        through = jnp.exp2(total)
        colours = [colours[c] + through * parts[d, c] for c in range(3)]
        total = total + parts[d, 3]
    for c in range(3):
        out[c] = colours[c]
    out[3] = 1.0 - jnp.exp2(total)


def composite(parts):
    return pl.pallas_call(
        composite_kernel,
        out_shape=jax.ShapeDtypeStruct(parts.shape[1:], jnp.float32),
    )(parts)


def neighbours(axis, low, high):
    size = lax.axis_size(axis)
    up = [(i, i + 1) for i in range(size - 1)]
    down = [(j, i) for i, j in up]
    return lax.ppermute(high, axis, up), lax.ppermute(low, axis, down)


def local(density, occupancy, light_dir, palette):
    planes, columns, rows = density.shape
    slabs = lax.axis_size("depth")
    devices = lax.axis_size("cols")
    zlow, zhigh = neighbours("depth", density[0], density[-1])
    xlow, xhigh = neighbours("cols", density[:, 0, :], density[:, -1, :])
    scale = -3.0 / (planes * slabs)
    occ = jnp.repeat(occupancy.astype(jnp.float32) * scale, rows // occupancy.shape[2], axis=2)
    parts = render(density, occ, light_dir, palette, zlow, zhigh, xlow, xhigh, slabs)
    parts = lax.all_to_all(parts, "depth", 0, 0, tiled=True)
    pixels = composite(parts)
    spread = jnp.broadcast_to(pixels[None], (devices,) + pixels.shape)
    image = lax.all_to_all(spread, "cols", 0, 0, tiled=True)
    return image.transpose(1, 0, 3, 2).reshape(4, devices * columns, rows // slabs)


def solution(mesh):
    placed = (P("depth", "cols", None), P("depth", "cols", None), P(), P())
    return jax.shard_map(
        local, mesh=mesh, in_specs=placed, out_specs=P(None, None, "depth"), check_vma=False
    )
```

```python
import jax
import jax.numpy as jnp
from jax import lax
from jax.experimental import pallas as pl
from jax.experimental.pallas import tpu as pltpu
from jax.sharding import PartitionSpec as P

BX = 16
LOG2E = 1.4426950408889634
CODE_TOP = 65535.0
CODE_STEP = CODE_TOP / 24.0
INNER_LIMIT = 20 * 1024 * 1024
OUTER_LIMIT = 16 * 1024 * 1024


def difference_matrix(rows):
    row = lax.broadcasted_iota(jnp.int32, (rows, rows), 0)
    col = lax.broadcasted_iota(jnp.int32, (rows, rows), 1)
    ahead = (row == col + 1).astype(jnp.float32)
    behind = (row + 1 == col).astype(jnp.float32)
    return (ahead - behind).astype(jnp.bfloat16)


def occupied_row(occ, zb, xb, rows, scale):
    parts = occ.shape[1]
    lane = lax.broadcasted_iota(jnp.int32, (BX, rows), 1)
    value = jnp.broadcast_to(occ[zb, parts - 1, xb], (BX, rows))
    for part in range(parts - 2, -1, -1):
        value = jnp.where(lane < (part + 1) * (rows // parts), occ[zb, part, xb], value)
    return value.astype(jnp.float32) * scale


def shade_terms(v, gz, gx, gy, light):
    norm = lax.rsqrt((gz * gz + gx * gx) + (gy * gy + 4.0))
    facing = (gz * light[0] + gx * light[1]) + gy * light[2]
    return jnp.abs(jnp.tanh(facing * norm)) + 3.0 / 7.0


def optical_term(v, coeff):
    return jnp.log2(1.0 + jnp.exp2(v * coeff[3][0] + coeff[3][1]))


def coefficients(pal):
    coeff = [(0.5 * pal[0, c], 0.5 * pal[1, c]) for c in range(3)]
    return coeff + [(pal[0, 3] * LOG2E, pal[1, 3] * LOG2E)]


def march(field, at, gradient, scale_of, light, coeff, planes, group, rows, ends):
    f32 = jnp.float32
    lights = [light[i] for i in range(3)]

    def body(k, carry):
        total, through, red, green, blue, white = carry
        zb = planes // group - 1 - k
        scale = scale_of(zb)
        base = zb * group
        gys = gradient(base)
        for zi in range(group - 1, -1, -1):
            z = base + zi
            v = field[z + 1, pl.ds(at + 1, BX), :]
            gz = field[z + 2, pl.ds(at + 1, BX), :] - field[z, pl.ds(at + 1, BX), :]
            gx = field[z + 1, pl.ds(at + 2, BX), :] - field[z + 1, pl.ds(at, BX), :]
            gy = gys[zi * BX:(zi + 1) * BX]
            total = total + scale * optical_term(v, coeff)
            beyond = jnp.exp2(total)
            weight = (through - beyond) * shade_terms(v, gz, gx, gy, lights)
            if not ends and zi == 0:
                weight = weight * (zb > 0).astype(f32)
            if not ends and zi == group - 1:
                weight = weight * (k > 0).astype(f32)
            through = beyond
            red = red + weight * jnp.tanh(v * coeff[0][0] + coeff[0][1])
            green = green + weight * jnp.tanh(v * coeff[1][0] + coeff[1][1])
            blue = blue + weight * jnp.tanh(v * coeff[2][0] + coeff[2][1])
            white = white + weight
        return total, through, red, green, blue, white

    zero = jnp.zeros((BX, rows), f32)
    total, _, red, green, blue, white = lax.fori_loop(
        0, planes // group, body, (zero, zero + 1.0, zero, zero, zero, zero)
    )
    return [0.35 * (white + red), 0.35 * (white + green), 0.35 * (white + blue), total]


def inner_kernel(scale, light, pal, occ, density, image, field, diff):
    planes, columns, rows = density.shape
    group = planes // occ.shape[0]
    diff[...] = difference_matrix(rows)
    field[0] = jnp.zeros((columns, rows), jnp.float32)
    field[planes + 1] = jnp.zeros((columns, rows), jnp.float32)

    @pl.loop(0, planes // 4)
    def _(k):
        for j in range(4):
            field[4 * k + j + 1] = density[4 * k + j].astype(jnp.float32)

    coeff = coefficients(pal)

    @pl.loop(1, columns // BX - 1)
    def _(block):
        first = pl.multiple_of(block * BX, BX)

        def gradient(base):
            piece = density[pl.ds(base, group), pl.ds(first, BX), :].reshape(group * BX, rows)
            return jnp.dot(piece, diff[...], preferred_element_type=jnp.float32)

        sums = march(
            field, first - 1, gradient, lambda zb: occupied_row(occ, zb, block, rows, scale),
            light, coeff, planes, group, rows, False,
        )
        for c in range(4):
            image[c, pl.ds(first, BX), :] = sums[c]


def outer_kernel(scale, light, pal, occ, density, image, zlow, zhigh, xlow, xhigh, out,
                 field, edge, whole):
    planes, columns, rows = density.shape
    group = planes // occ.shape[0]
    f32 = jnp.float32
    diff = difference_matrix(rows)
    coeff = coefficients(pal)
    last = columns // BX - 1
    lights = [light[i] for i in range(3)]
    whole[...] = image[...]

    for block, halo in ((0, xlow), (last, xhigh)):
        first = block * BX
        field[pl.ds(1, planes), 8:8 + BX, :] = density[:, first:first + BX, :].astype(f32)
        field[0, 8:8 + BX, :] = zlow[first:first + BX, :].astype(f32)
        field[planes + 1, 8:8 + BX, :] = zhigh[first:first + BX, :].astype(f32)
        edge[...] = halo[...].astype(f32)
        if block == 0:
            field[pl.ds(1, planes), 8 + BX:16 + BX, :] = density[:, BX:BX + 8, :].astype(f32)
            spot = 0
        else:
            field[pl.ds(1, planes), 0:8, :] = density[:, first - 8:first, :].astype(f32)
            spot = 8 + BX

        @pl.loop(0, planes // 8)
        def _(k):
            for j in range(8):
                row = edge[pl.ds(8 * k + j, 1), :]
                field[8 * k + j + 1, spot:spot + 8, :] = jnp.broadcast_to(row, (8, rows))

        def gradient(base):
            piece = density[pl.ds(base, group), first:first + BX, :].reshape(group * BX, rows)
            return jnp.dot(piece, diff, preferred_element_type=f32)

        sums = march(
            field, 7, gradient, lambda zb: occupied_row(occ, zb, block, rows, scale),
            light, coeff, planes, group, rows, True,
        )
        for c in range(4):
            whole[c, first:first + BX, :] = sums[c]

    for block in range(1, last):
        at = slice(block * BX, (block + 1) * BX)
        total = whole[3, at, :]
        for z in (planes - 1, 0):
            plane = density[z].astype(f32)
            v = plane[at]
            if z == 0:
                gz = density[1, at, :].astype(f32) - zlow[at, :].astype(f32)
            else:
                gz = zhigh[at, :].astype(f32) - density[z - 1, at, :].astype(f32)
            gx = plane[at.start + 1:at.stop + 1] - plane[at.start - 1:at.stop - 1]
            gy = jnp.dot(density[z, at, :], diff, preferred_element_type=f32)
            here = occupied_row(occ, z // group, block, rows, scale) * optical_term(v, coeff)
            if z == 0:
                weight = jnp.exp2(total - here) - jnp.exp2(total)
            else:
                weight = 1.0 - jnp.exp2(here)
            weight = weight * shade_terms(v, gz, gx, gy, lights) * 0.35
            for c in range(3):
                whole[c, at, :] += weight + weight * jnp.tanh(v * coeff[c][0] + coeff[c][1])

    slabs, _, share, _ = out.shape
    for c in range(4):
        turned = whole[c].T
        for d in range(slabs):
            out[d, c] = turned[d * share:(d + 1) * share, :]


def smem():
    return pl.BlockSpec(memory_space=pltpu.SMEM)


def vmem():
    return pl.BlockSpec(memory_space=pltpu.VMEM)


def render_inner(density, occ, light_dir, pal, scale):
    planes, columns, rows = density.shape
    return pl.pallas_call(
        lambda *refs: inner_kernel(scale, *refs),
        in_specs=[smem(), smem(), smem(), vmem()],
        out_specs=vmem(),
        out_shape=jax.ShapeDtypeStruct((4, columns, rows), jnp.float32),
        scratch_shapes=[
            pltpu.VMEM((planes + 2, columns, rows), jnp.float32),
            pltpu.VMEM((rows, rows), jnp.bfloat16),
        ],
        cost_estimate=pl.CostEstimate(
            flops=40 * density.size, bytes_accessed=2 * density.size,
            transcendentals=8 * density.size,
        ),
        compiler_params=pltpu.CompilerParams(vmem_limit_bytes=INNER_LIMIT),
    )(light_dir, pal, occ, density)


def render_outer(density, occ, light_dir, pal, image, halos, scale, slabs):
    planes, columns, rows = density.shape
    return pl.pallas_call(
        lambda *refs: outer_kernel(scale, *refs),
        in_specs=[smem(), smem(), smem()] + [vmem()] * 6,
        out_specs=vmem(),
        out_shape=jax.ShapeDtypeStruct((slabs, 4, rows // slabs, columns), jnp.float32),
        scratch_shapes=[
            pltpu.VMEM((planes + 2, BX + 16, rows), jnp.float32),
            pltpu.VMEM((planes, rows), jnp.float32),
            pltpu.VMEM((4, columns, rows), jnp.float32),
        ],
        compiler_params=pltpu.CompilerParams(vmem_limit_bytes=OUTER_LIMIT),
    )(light_dir, pal, occ, density, image, *halos)


def composite_kernel(parts, out):
    slabs = parts.shape[0]
    total = parts[slabs - 1, 3]
    colours = [parts[slabs - 1, c] for c in range(3)]
    for d in range(slabs - 2, -1, -1):
        through = jnp.exp2(total)
        colours = [colours[c] + through * parts[d, c] for c in range(3)]
        total = total + parts[d, 3]
    colours.append(1.0 - jnp.exp2(total))
    for c in range(4):
        level = jnp.log2(jnp.maximum(colours[c], 2.0 ** -24))
        code = (level * CODE_STEP + (CODE_TOP + 0.5)).astype(jnp.int32) - 32768
        code = code.astype(jnp.int16)
        for k in range(out.shape[0]):
            out[k, c] = code


def composite(parts, devices):
    return pl.pallas_call(
        composite_kernel,
        out_shape=jax.ShapeDtypeStruct((devices,) + parts.shape[1:], jnp.int16),
    )(parts)


def decode_kernel(codes, out):
    devices, _, share, columns = codes.shape
    for k in range(devices):
        code = codes[k, 0].astype(jnp.int32) + 32768
        value = jnp.exp2((code.astype(jnp.float32) - CODE_TOP) * (1.0 / CODE_STEP))
        out[0, :, k * columns:(k + 1) * columns] = jnp.where(code > 0, value, 0.0)


def decode(codes):
    devices, channels, share, columns = codes.shape
    return pl.pallas_call(
        decode_kernel,
        grid=(channels,),
        in_specs=[pl.BlockSpec((devices, 1, share, columns), lambda c: (0, c, 0, 0))],
        out_specs=pl.BlockSpec((1, share, devices * columns), lambda c: (c, 0, 0)),
        out_shape=jax.ShapeDtypeStruct((channels, share, devices * columns), jnp.float32),
    )(codes)


def neighbours(axis, low, high):
    size = lax.axis_size(axis)
    up = [(i, i + 1) for i in range(size - 1)]
    down = [(j, i) for i, j in up]
    return lax.ppermute(high, axis, up), lax.ppermute(low, axis, down)


def local(density, occupancy, light_dir, palette):
    planes, columns, rows = density.shape
    slabs = lax.axis_size("depth")
    devices = lax.axis_size("cols")
    scale = -3.0 / (planes * slabs)
    xhalo = neighbours("cols", density[:, 0, :], density[:, -1, :])
    zhalo = neighbours("depth", density[0], density[-1])
    occ = occupancy.transpose(0, 2, 1)
    pal = palette.T
    image = render_inner(density, occ, light_dir, pal, scale)
    parts = render_outer(density, occ, light_dir, pal, image, zhalo + xhalo, scale, slabs)
    parts = lax.all_to_all(parts, "depth", 0, 0, tiled=True)
    codes = composite(parts, devices)
    codes = lax.all_to_all(codes, "cols", 0, 0, tiled=True)
    return decode(codes).transpose(0, 2, 1)


def solution(mesh):
    placed = (P("depth", "cols", None), P("depth", "cols", None), P(), P())
    return jax.shard_map(
        local, mesh=mesh, in_specs=placed, out_specs=P(None, None, "depth"), check_vma=False
    )
```

```python
import jax
import jax.numpy as jnp
from jax import lax
from jax.experimental import pallas as pl
from jax.experimental.pallas import tpu as pltpu
from jax.sharding import PartitionSpec as P

BX = 16
LOG2E = 1.4426950408889634
CODE_TOP = 65535.0
CODE_STEP = CODE_TOP / 24.0
PREPARE_LIMIT = 24 * 1024 * 1024
RENDER_LIMIT = 24 * 1024 * 1024


def difference_matrix(rows):
    row = lax.broadcasted_iota(jnp.int32, (rows, rows), 0)
    col = lax.broadcasted_iota(jnp.int32, (rows, rows), 1)
    ahead = (row == col + 1).astype(jnp.float32)
    behind = (row + 1 == col).astype(jnp.float32)
    return (ahead - behind).astype(jnp.bfloat16)


def occupied_row(occ, zb, xb, rows, scale):
    parts = occ.shape[1]
    lane = lax.broadcasted_iota(jnp.int32, (BX, rows), 1)
    value = jnp.broadcast_to(occ[zb, parts - 1, xb], (BX, rows))
    for part in range(parts - 2, -1, -1):
        value = jnp.where(lane < (part + 1) * (rows // parts), occ[zb, part, xb], value)
    return value.astype(jnp.float32) * scale


def prepare_kernel(density, field, slope, diff):
    planes, columns, rows = density.shape
    diff[...] = difference_matrix(rows)

    @pl.loop(0, planes // 4)
    def _(k):
        at = pl.ds(4 * k, 4)
        part = density[at]
        field[at, 8:8 + columns, :] = part.astype(jnp.float32)
        step = jnp.dot(part.reshape(4 * columns, rows), diff[...],
                       preferred_element_type=jnp.float32)
        slope[at] = step.reshape(4, columns, rows)


def prepare(density):
    planes, columns, rows = density.shape
    vmem = pl.BlockSpec(memory_space=pltpu.VMEM)
    return pl.pallas_call(
        prepare_kernel,
        in_specs=[vmem],
        out_specs=[vmem] * 2,
        out_shape=[
            jax.ShapeDtypeStruct((planes, columns + 16, rows), jnp.float32),
            jax.ShapeDtypeStruct(density.shape, jnp.float32),
        ],
        scratch_shapes=[pltpu.VMEM((rows, rows), jnp.bfloat16)],
        cost_estimate=pl.CostEstimate(
            flops=2 * density.size * rows, bytes_accessed=10 * density.size, transcendentals=0
        ),
        compiler_params=pltpu.CompilerParams(vmem_limit_bytes=PREPARE_LIMIT),
    )(density)


def render_kernel(depth_scale, light_dir, pal, occ, field, slope, zlow, zhigh, xlow, xhigh,
                  out, edge, image):
    planes, columns, rows = slope.shape
    group = planes // occ.shape[0]
    f32 = jnp.float32
    edge[0] = xlow[...].astype(f32)
    edge[1] = xhigh[...].astype(f32)
    sublane = lax.broadcasted_iota(jnp.int32, (BX, rows), 0)
    light = [light_dir[i] for i in range(3)]
    half = [(0.5 * pal[0, c], 0.5 * pal[1, c]) for c in range(3)]
    extinct = (pal[0, 3] * LOG2E, pal[1, 3] * LOG2E)
    span = 2 * group
    steps = planes // span

    def march(block, outer):
        first = pl.multiple_of(block * BX, BX)
        lowest = (sublane == 0) & (block == 0)
        highest = (sublane == BX - 1) & (block != 0)

        def body(k, carry):
            total, through, red, green, blue, white = carry
            base = (steps - 1 - k) * span
            for zi in range(span - 1, -1, -1):
                if (zi + 1) % group == 0:
                    zb = base // group + zi // group
                    scale = occupied_row(occ, zb, block, rows, depth_scale)
                z = base + zi
                v = field[z, pl.ds(first + 8, BX), :]
                if zi == span - 1:
                    ahead = field[jnp.minimum(z + 1, planes - 1), pl.ds(first + 8, BX), :]
                    ahead = jnp.where(k == 0, zhigh[pl.ds(first, BX), :].astype(f32), ahead)
                else:
                    ahead = field[z + 1, pl.ds(first + 8, BX), :]
                if zi == 0:
                    behind = field[jnp.maximum(z - 1, 0), pl.ds(first + 8, BX), :]
                    ghost = zlow[pl.ds(first, BX), :].astype(f32)
                    behind = jnp.where(k == steps - 1, ghost, behind)
                else:
                    behind = field[z - 1, pl.ds(first + 8, BX), :]
                right = field[z, pl.ds(first + 9, BX), :]
                left = field[z, pl.ds(first + 7, BX), :]
                if outer:
                    right = jnp.where(highest, edge[1, pl.ds(z, 1), :], right)
                    left = jnp.where(lowest, edge[0, pl.ds(z, 1), :], left)
                gz = ahead - behind
                gx = right - left
                gy = slope[z, pl.ds(first, BX), :]
                norm = lax.rsqrt((gz * gz + gx * gx) + (gy * gy + 4.0))
                facing = (gz * light[0] + gx * light[1]) + gy * light[2]
                shade = jnp.abs(jnp.tanh(facing * norm)) + 3.0 / 7.0
                optical = jnp.log2(1.0 + jnp.exp2(v * extinct[0] + extinct[1]))
                total = total + scale * optical
                beyond = jnp.exp2(total)
                weight = (through - beyond) * shade
                through = beyond
                red = red + weight * jnp.tanh(v * half[0][0] + half[0][1])
                green = green + weight * jnp.tanh(v * half[1][0] + half[1][1])
                blue = blue + weight * jnp.tanh(v * half[2][0] + half[2][1])
                white = white + weight
            return total, through, red, green, blue, white

        zero = jnp.zeros((BX, rows), f32)
        total, _, red, green, blue, white = lax.fori_loop(
            0, steps, body, (zero, zero + 1.0, zero, zero, zero, zero)
        )
        at = pl.ds(first, BX)
        image[0, at, :] = 0.35 * (white + red)
        image[1, at, :] = 0.35 * (white + green)
        image[2, at, :] = 0.35 * (white + blue)
        image[3, at, :] = total

    last = columns // BX - 1

    @pl.loop(0, 2)
    def _(side):
        march(side * last, True)

    @pl.loop(1, last)
    def _(block):
        march(block, False)

    slabs, _, share, _ = out.shape
    for c in range(4):
        turned = image[c].T
        for d in range(slabs):
            out[d, c] = turned[d * share:(d + 1) * share, :]


def render(prepared, occ, light_dir, pal, halos, depth_scale, slabs):
    field, slope = prepared
    planes, columns, rows = slope.shape
    smem = pl.BlockSpec(memory_space=pltpu.SMEM)
    vmem = pl.BlockSpec(memory_space=pltpu.VMEM)
    return pl.pallas_call(
        lambda *refs: render_kernel(depth_scale, *refs),
        in_specs=[smem] * 3 + [vmem] * 6,
        out_specs=vmem,
        out_shape=jax.ShapeDtypeStruct((slabs, 4, rows // slabs, columns), jnp.float32),
        scratch_shapes=[
            pltpu.VMEM((2, planes, rows), jnp.float32),
            pltpu.VMEM((4, columns, rows), jnp.float32),
        ],
        compiler_params=pltpu.CompilerParams(vmem_limit_bytes=RENDER_LIMIT),
    )(light_dir, pal, occ, field, slope, *halos)


def composite(parts):
    slabs = parts.shape[0]
    colours, total = parts[slabs - 1, :3], parts[slabs - 1, 3:]
    for d in range(slabs - 2, -1, -1):
        colours = colours + jnp.exp2(total) * parts[d, :3]
        total = total + parts[d, 3:]
    return jnp.concatenate([colours, 1.0 - jnp.exp2(total)], axis=0)


def encode(pixels):
    level = jnp.log2(jnp.maximum(pixels, 2.0 ** -24))
    code = (level * CODE_STEP + (CODE_TOP + 0.5)).astype(jnp.int32) - 32768
    return code.astype(jnp.int16)


def decode(codes):
    code = codes.astype(jnp.float32)
    level = code * (1.0 / CODE_STEP) + (32768.0 - CODE_TOP) / CODE_STEP
    return jnp.where(code > -32768.0, jnp.exp2(level), 0.0)


def neighbours(axis, low, high):
    size = lax.axis_size(axis)
    up = [(i, i + 1) for i in range(size - 1)]
    down = [(j, i) for i, j in up]
    return lax.ppermute(high, axis, up), lax.ppermute(low, axis, down)


def local(density, occupancy, light_dir, palette):
    planes, columns, rows = density.shape
    slabs = lax.axis_size("depth")
    devices = lax.axis_size("cols")
    zhalo = neighbours("depth", density[0], density[-1])
    xhalo = neighbours("cols", density[:, 0, :], density[:, -1, :])
    occ = occupancy.transpose(0, 2, 1)
    depth_scale = -3.0 / (planes * slabs)
    parts = render(prepare(density), occ, light_dir, palette.T, zhalo + xhalo, depth_scale, slabs)
    parts = lax.all_to_all(parts, "depth", 0, 0, tiled=True)
    codes = encode(composite(parts))
    codes = jnp.broadcast_to(codes[None], (devices,) + codes.shape)
    codes = lax.all_to_all(codes, "cols", 0, 0, tiled=True)
    return decode(codes).transpose(1, 0, 3, 2).reshape(4, devices * columns, rows // slabs)


def solution(mesh):
    placed = (P("depth", "cols", None), P("depth", "cols", None), P(), P())
    return jax.shard_map(
        local, mesh=mesh, in_specs=placed, out_specs=P(None, None, "depth"), check_vma=False
    )
```

```python
import jax
import jax.numpy as jnp
from jax import lax
from jax.experimental import pallas as pl
from jax.experimental.pallas import tpu as pltpu
from jax.sharding import PartitionSpec as P

BX = 16
LOG2E = 1.4426950408889634
CODE_TOP = 65535.0
CODE_STEP = CODE_TOP / 24.0
PREPARE_LIMIT = 24 * 1024 * 1024
RENDER_LIMIT = 24 * 1024 * 1024


def difference_matrix(rows):
    row = lax.broadcasted_iota(jnp.int32, (rows, rows), 0)
    col = lax.broadcasted_iota(jnp.int32, (rows, rows), 1)
    ahead = (row == col + 1).astype(jnp.float32)
    behind = (row + 1 == col).astype(jnp.float32)
    return (ahead - behind).astype(jnp.bfloat16)


def occupied_row(occ, zb, xb, rows, scale):
    parts = occ.shape[1]
    lane = lax.broadcasted_iota(jnp.int32, (BX, rows), 1)
    value = jnp.broadcast_to(occ[zb, parts - 1, xb], (BX, rows))
    for part in range(parts - 2, -1, -1):
        value = jnp.where(lane < (part + 1) * (rows // parts), occ[zb, part, xb], value)
    return value.astype(jnp.float32) * scale


def prepare_kernel(density, field, slope, diff):
    planes, columns, rows = density.shape
    diff[...] = difference_matrix(rows)

    @pl.loop(0, planes // 16)
    def _(k):
        at = pl.ds(16 * k, 16)
        part = density[at]
        field[at, 8:8 + columns, :] = part.astype(jnp.float32)
        step = jnp.dot(part.reshape(16 * columns, rows), diff[...],
                       preferred_element_type=jnp.float32)
        slope[at] = step.reshape(16, columns, rows)


def prepare(density):
    planes, columns, rows = density.shape
    vmem = pl.BlockSpec(memory_space=pltpu.VMEM)
    return pl.pallas_call(
        prepare_kernel,
        in_specs=[vmem],
        out_specs=[vmem] * 2,
        out_shape=[
            jax.ShapeDtypeStruct((planes, columns + 16, rows), jnp.float32),
            jax.ShapeDtypeStruct(density.shape, jnp.float32),
        ],
        scratch_shapes=[pltpu.VMEM((rows, rows), jnp.bfloat16)],
        cost_estimate=pl.CostEstimate(
            flops=2 * density.size * rows, bytes_accessed=10 * density.size, transcendentals=0
        ),
        compiler_params=pltpu.CompilerParams(vmem_limit_bytes=PREPARE_LIMIT),
    )(density)


def render_kernel(depth_scale, light_dir, pal, occ, field, slope, zlow, zhigh, xlow, xhigh,
                  out, edge, image):
    planes, columns, rows = slope.shape
    group = planes // occ.shape[0]
    f32 = jnp.float32
    edge[0] = xlow[...].astype(f32)
    edge[1] = xhigh[...].astype(f32)
    sublane = lax.broadcasted_iota(jnp.int32, (BX, rows), 0)
    light = [light_dir[i] for i in range(3)]
    half = [(0.5 * pal[0, c], 0.5 * pal[1, c]) for c in range(3)]
    extinct = (pal[0, 3] * LOG2E, pal[1, 3] * LOG2E)
    span = 2 * group
    steps = planes // span

    def march(block, outer):
        first = pl.multiple_of(block * BX, BX)
        lowest = (sublane == 0) & (block == 0)
        highest = (sublane == BX - 1) & (block != 0)

        def body(k, carry):
            total, through, red, green, blue, white = carry
            base = (steps - 1 - k) * span
            for zi in range(span - 1, -1, -1):
                if (zi + 1) % group == 0:
                    zb = base // group + zi // group
                    scale = occupied_row(occ, zb, block, rows, depth_scale)
                z = base + zi
                v = field[z, pl.ds(first + 8, BX), :]
                if zi == span - 1:
                    ahead = field[jnp.minimum(z + 1, planes - 1), pl.ds(first + 8, BX), :]
                    ahead = jnp.where(k == 0, zhigh[pl.ds(first, BX), :].astype(f32), ahead)
                else:
                    ahead = field[z + 1, pl.ds(first + 8, BX), :]
                if zi == 0:
                    behind = field[jnp.maximum(z - 1, 0), pl.ds(first + 8, BX), :]
                    ghost = zlow[pl.ds(first, BX), :].astype(f32)
                    behind = jnp.where(k == steps - 1, ghost, behind)
                else:
                    behind = field[z - 1, pl.ds(first + 8, BX), :]
                right = field[z, pl.ds(first + 9, BX), :]
                left = field[z, pl.ds(first + 7, BX), :]
                if outer:
                    right = jnp.where(highest, edge[1, pl.ds(z, 1), :], right)
                    left = jnp.where(lowest, edge[0, pl.ds(z, 1), :], left)
                gz = ahead - behind
                gx = right - left
                gy = slope[z, pl.ds(first, BX), :]
                norm = lax.rsqrt((gz * gz + gx * gx) + (gy * gy + 4.0))
                facing = (gz * light[0] + gx * light[1]) + gy * light[2]
                shade = jnp.abs(jnp.tanh(facing * norm)) + 3.0 / 7.0
                optical = jnp.log2(1.0 + jnp.exp2(v * extinct[0] + extinct[1]))
                total = total + scale * optical
                beyond = jnp.exp2(total)
                weight = (through - beyond) * shade
                through = beyond
                red = red + weight * jnp.tanh(v * half[0][0] + half[0][1])
                green = green + weight * jnp.tanh(v * half[1][0] + half[1][1])
                blue = blue + weight * jnp.tanh(v * half[2][0] + half[2][1])
                white = white + weight
            return total, through, red, green, blue, white

        zero = jnp.zeros((BX, rows), f32)
        total, _, red, green, blue, white = lax.fori_loop(
            0, steps, body, (zero, zero + 1.0, zero, zero, zero, zero)
        )
        at = pl.ds(first, BX)
        image[0, at, :] = 0.35 * (white + red)
        image[1, at, :] = 0.35 * (white + green)
        image[2, at, :] = 0.35 * (white + blue)
        image[3, at, :] = total

    last = columns // BX - 1

    @pl.loop(0, 2)
    def _(side):
        march(side * last, True)

    @pl.loop(1, last)
    def _(block):
        march(block, False)

    slabs, _, share, _ = out.shape
    for c in range(4):
        turned = image[c].T
        for d in range(slabs):
            out[d, c] = turned[d * share:(d + 1) * share, :]


def render(prepared, occ, light_dir, pal, halos, depth_scale, slabs):
    field, slope = prepared
    planes, columns, rows = slope.shape
    smem = pl.BlockSpec(memory_space=pltpu.SMEM)
    vmem = pl.BlockSpec(memory_space=pltpu.VMEM)
    return pl.pallas_call(
        lambda *refs: render_kernel(depth_scale, *refs),
        in_specs=[smem] * 3 + [vmem] * 6,
        out_specs=vmem,
        out_shape=jax.ShapeDtypeStruct((slabs, 4, rows // slabs, columns), jnp.float32),
        scratch_shapes=[
            pltpu.VMEM((2, planes, rows), jnp.float32),
            pltpu.VMEM((4, columns, rows), jnp.float32),
        ],
        compiler_params=pltpu.CompilerParams(vmem_limit_bytes=RENDER_LIMIT),
    )(light_dir, pal, occ, field, slope, *halos)


def composite(parts):
    slabs = parts.shape[0]
    colours, total = parts[slabs - 1, :3], parts[slabs - 1, 3:]
    for d in range(slabs - 2, -1, -1):
        colours = colours + jnp.exp2(total) * parts[d, :3]
        total = total + parts[d, 3:]
    return jnp.concatenate([colours, 1.0 - jnp.exp2(total)], axis=0)


def encode(pixels):
    level = jnp.log2(jnp.maximum(pixels, 2.0 ** -24))
    code = (level * CODE_STEP + (CODE_TOP + 0.5)).astype(jnp.int32) - 32768
    return code.astype(jnp.int16)


def decode(codes):
    code = codes.astype(jnp.float32)
    level = code * (1.0 / CODE_STEP) + (32768.0 - CODE_TOP) / CODE_STEP
    return jnp.where(code > -32768.0, jnp.exp2(level), 0.0)


def neighbours(axis, low, high):
    size = lax.axis_size(axis)
    up = [(i, i + 1) for i in range(size - 1)]
    down = [(j, i) for i, j in up]
    return lax.ppermute(high, axis, up), lax.ppermute(low, axis, down)


def local(density, occupancy, light_dir, palette):
    planes, columns, rows = density.shape
    slabs = lax.axis_size("depth")
    devices = lax.axis_size("cols")
    zhalo = neighbours("depth", density[0], density[-1])
    xhalo = neighbours("cols", density[:, 0, :], density[:, -1, :])
    occ = occupancy.transpose(0, 2, 1)
    depth_scale = -3.0 / (planes * slabs)
    parts = render(prepare(density), occ, light_dir, palette.T, zhalo + xhalo, depth_scale, slabs)
    parts = lax.all_to_all(parts, "depth", 0, 0, tiled=True)
    codes = encode(composite(parts))
    codes = jnp.broadcast_to(codes[None], (devices,) + codes.shape)
    codes = lax.all_to_all(codes, "cols", 0, 0, tiled=True)
    return decode(codes).transpose(1, 0, 3, 2).reshape(4, devices * columns, rows // slabs)


def solution(mesh):
    placed = (P("depth", "cols", None), P("depth", "cols", None), P(), P())
    return jax.shard_map(
        local, mesh=mesh, in_specs=placed, out_specs=P(None, None, "depth"), check_vma=False
    )
```

```python
import jax
import jax.numpy as jnp
from jax import lax
from jax.experimental import pallas as pl
from jax.experimental.pallas import tpu as pltpu
from jax.sharding import PartitionSpec as P

BX = 16
LOG2E = 1.4426950408889634
CODE_TOP = 65535.0
CODE_STEP = CODE_TOP / 24.0
PREPARE_LIMIT = 24 * 1024 * 1024
RENDER_LIMIT = 24 * 1024 * 1024


def difference_matrix(rows):
    row = lax.broadcasted_iota(jnp.int32, (rows, rows), 0)
    col = lax.broadcasted_iota(jnp.int32, (rows, rows), 1)
    ahead = (row == col + 1).astype(jnp.float32)
    behind = (row + 1 == col).astype(jnp.float32)
    return (ahead - behind).astype(jnp.bfloat16)


def occupied_row(occ, zb, xb, rows, scale):
    parts = occ.shape[1]
    lane = lax.broadcasted_iota(jnp.int32, (BX, rows), 1)
    value = jnp.broadcast_to(occ[zb, parts - 1, xb], (BX, rows))
    for part in range(parts - 2, -1, -1):
        value = jnp.where(lane < (part + 1) * (rows // parts), occ[zb, part, xb], value)
    return value.astype(jnp.float32) * scale


def prepare_kernel(density, field, slope, diff):
    planes, columns, rows = density.shape
    diff[...] = difference_matrix(rows)

    @pl.loop(0, planes // 16)
    def _(k):
        at = pl.ds(16 * k, 16)
        part = density[at]
        field[at, 8:8 + columns, :] = part.astype(jnp.float32)
        step = jnp.dot(part.reshape(16 * columns, rows), diff[...],
                       preferred_element_type=jnp.float32)
        slope[at] = step.reshape(16, columns, rows)


def prepare(density):
    planes, columns, rows = density.shape
    vmem = pl.BlockSpec(memory_space=pltpu.VMEM)
    return pl.pallas_call(
        prepare_kernel,
        in_specs=[vmem],
        out_specs=[vmem] * 2,
        out_shape=[
            jax.ShapeDtypeStruct((planes, columns + 16, rows), jnp.float32),
            jax.ShapeDtypeStruct(density.shape, jnp.float32),
        ],
        scratch_shapes=[pltpu.VMEM((rows, rows), jnp.bfloat16)],
        cost_estimate=pl.CostEstimate(
            flops=2 * density.size * rows, bytes_accessed=10 * density.size, transcendentals=0
        ),
        compiler_params=pltpu.CompilerParams(vmem_limit_bytes=PREPARE_LIMIT),
    )(density)


def render_kernel(depth_scale, light_dir, pal, occ, field, slope, zlow, zhigh, xlow, xhigh,
                  out, edge, image):
    planes, columns, rows = slope.shape
    group = planes // occ.shape[0]
    f32 = jnp.float32
    edge[0] = xlow[...].astype(f32)
    edge[1] = xhigh[...].astype(f32)
    sublane = lax.broadcasted_iota(jnp.int32, (BX, rows), 0)
    light = [light_dir[i] for i in range(3)]
    half = [(0.5 * pal[0, c], 0.5 * pal[1, c]) for c in range(3)]
    extinct = (pal[0, 3] * LOG2E, pal[1, 3] * LOG2E)
    span = 2 * group
    steps = planes // span

    def march(block, outer):
        first = pl.multiple_of(block * BX, BX)
        lowest = (sublane == 0) & (block == 0)
        highest = (sublane == BX - 1) & (block != 0)

        def body(k, carry):
            total, through, red, green, blue, white = carry
            base = (steps - 1 - k) * span
            for zi in range(span - 1, -1, -1):
                if (zi + 1) % group == 0:
                    zb = base // group + zi // group
                    scale = occupied_row(occ, zb, block, rows, depth_scale)
                z = base + zi
                v = field[z, pl.ds(first + 8, BX), :]
                if zi == span - 1:
                    ahead = field[jnp.minimum(z + 1, planes - 1), pl.ds(first + 8, BX), :]
                    ahead = jnp.where(k == 0, zhigh[pl.ds(first, BX), :].astype(f32), ahead)
                else:
                    ahead = field[z + 1, pl.ds(first + 8, BX), :]
                if zi == 0:
                    behind = field[jnp.maximum(z - 1, 0), pl.ds(first + 8, BX), :]
                    ghost = zlow[pl.ds(first, BX), :].astype(f32)
                    behind = jnp.where(k == steps - 1, ghost, behind)
                else:
                    behind = field[z - 1, pl.ds(first + 8, BX), :]
                right = field[z, pl.ds(first + 9, BX), :]
                left = field[z, pl.ds(first + 7, BX), :]
                if outer:
                    right = jnp.where(highest, edge[1, pl.ds(z, 1), :], right)
                    left = jnp.where(lowest, edge[0, pl.ds(z, 1), :], left)
                gz = ahead - behind
                gx = right - left
                gy = slope[z, pl.ds(first, BX), :]
                norm = lax.rsqrt((gz * gz + gx * gx) + (gy * gy + 4.0))
                facing = (gz * light[0] + gx * light[1]) + gy * light[2]
                shade = jnp.abs(jnp.tanh(facing * norm)) + 3.0 / 7.0
                optical = jnp.log2(1.0 + jnp.exp2(v * extinct[0] + extinct[1]))
                total = total + scale * optical
                beyond = jnp.exp2(total)
                weight = (through - beyond) * shade
                through = beyond
                red = red + weight * jnp.tanh(v * half[0][0] + half[0][1])
                green = green + weight * jnp.tanh(v * half[1][0] + half[1][1])
                blue = blue + weight * jnp.tanh(v * half[2][0] + half[2][1])
                white = white + weight
            return total, through, red, green, blue, white

        zero = jnp.zeros((BX, rows), f32)
        total, _, red, green, blue, white = lax.fori_loop(
            0, steps, body, (zero, zero + 1.0, zero, zero, zero, zero)
        )
        at = pl.ds(first, BX)
        image[0, at, :] = 0.35 * (white + red)
        image[1, at, :] = 0.35 * (white + green)
        image[2, at, :] = 0.35 * (white + blue)
        image[3, at, :] = total

    last = columns // BX - 1

    @pl.loop(0, 2)
    def _(side):
        march(side * last, True)

    @pl.loop(1, last)
    def _(block):
        march(block, False)

    slabs, _, share, _ = out.shape
    for c in range(4):
        turned = image[c].T
        for d in range(slabs):
            out[d, c] = turned[d * share:(d + 1) * share, :]


def render(prepared, occ, light_dir, pal, halos, depth_scale, slabs):
    field, slope = prepared
    planes, columns, rows = slope.shape
    smem = pl.BlockSpec(memory_space=pltpu.SMEM)
    vmem = pl.BlockSpec(memory_space=pltpu.VMEM)
    return pl.pallas_call(
        lambda *refs: render_kernel(depth_scale, *refs),
        in_specs=[smem] * 3 + [vmem] * 6,
        out_specs=vmem,
        out_shape=jax.ShapeDtypeStruct((slabs, 4, rows // slabs, columns), jnp.float32),
        scratch_shapes=[
            pltpu.VMEM((2, planes, rows), jnp.float32),
            pltpu.VMEM((4, columns, rows), jnp.float32),
        ],
        compiler_params=pltpu.CompilerParams(vmem_limit_bytes=RENDER_LIMIT),
    )(light_dir, pal, occ, field, slope, *halos)


def composite(parts):
    slabs = parts.shape[0]
    colours, total = parts[slabs - 1, :3], parts[slabs - 1, 3:]
    for d in range(slabs - 2, -1, -1):
        colours = colours + jnp.exp2(total) * parts[d, :3]
        total = total + parts[d, 3:]
    return jnp.concatenate([colours, 1.0 - jnp.exp2(total)], axis=0)


def encode(pixels):
    level = jnp.log2(jnp.maximum(pixels, 2.0 ** -24))
    code = (level * CODE_STEP + (CODE_TOP + 0.5)).astype(jnp.int32) - 32768
    return code.astype(jnp.int16)


def decode(codes):
    code = codes.astype(jnp.float32)
    level = code * (1.0 / CODE_STEP) + (32768.0 - CODE_TOP) / CODE_STEP
    return jnp.where(code > -32768.0, jnp.exp2(level), 0.0)


def neighbours(axis, low, high):
    size = lax.axis_size(axis)
    odd = lax.axis_index(axis) % 2 == 1
    near = [pair for i in range(0, size - 1, 2) for pair in ((i, i + 1), (i + 1, i))]
    far = [pair for i in range(1, size - 1, 2) for pair in ((i, i + 1), (i + 1, i))]
    from_far = lax.ppermute(jnp.where(odd, high, low), axis, far)
    from_near = lax.ppermute(jnp.where(odd, low, high), axis, near)
    return jnp.where(odd, from_near, from_far), jnp.where(odd, from_far, from_near)


def local(density, occupancy, light_dir, palette):
    planes, columns, rows = density.shape
    slabs = lax.axis_size("depth")
    devices = lax.axis_size("cols")
    zhalo = neighbours("depth", density[0], density[-1])
    xhalo = neighbours("cols", density[:, 0, :], density[:, -1, :])
    occ = occupancy.transpose(0, 2, 1)
    depth_scale = -3.0 / (planes * slabs)
    parts = render(prepare(density), occ, light_dir, palette.T, zhalo + xhalo, depth_scale, slabs)
    parts = lax.all_to_all(parts, "depth", 0, 0, tiled=True)
    codes = encode(composite(parts))
    codes = jnp.broadcast_to(codes[None], (devices,) + codes.shape)
    codes = lax.all_to_all(codes, "cols", 0, 0, tiled=True)
    return decode(codes).transpose(1, 0, 3, 2).reshape(4, devices * columns, rows // slabs)


def solution(mesh):
    placed = (P("depth", "cols", None), P("depth", "cols", None), P(), P())
    return jax.shard_map(
        local, mesh=mesh, in_specs=placed, out_specs=P(None, None, "depth"), check_vma=False
    )
```

```python
import jax
import jax.numpy as jnp
from jax import lax
from jax.experimental import pallas as pl
from jax.experimental.pallas import tpu as pltpu
from jax.sharding import PartitionSpec as P

BX = 16
LOG2E = 1.4426950408889634
CODE_TOP = 65535.0
CODE_STEP = CODE_TOP / 24.0
FACES_LIMIT = 53 * 1024 * 1024
PREPARE_LIMIT = 24 * 1024 * 1024
RENDER_LIMIT = 24 * 1024 * 1024


def difference_matrix(rows):
    row = lax.broadcasted_iota(jnp.int32, (rows, rows), 0)
    col = lax.broadcasted_iota(jnp.int32, (rows, rows), 1)
    ahead = (row == col + 1).astype(jnp.float32)
    behind = (row + 1 == col).astype(jnp.float32)
    return (ahead - behind).astype(jnp.bfloat16)


def occupied_row(occ, zb, xb, rows, scale):
    parts = occ.shape[1]
    lane = lax.broadcasted_iota(jnp.int32, (BX, rows), 1)
    value = jnp.broadcast_to(occ[zb, parts - 1, xb], (BX, rows))
    for part in range(parts - 2, -1, -1):
        value = jnp.where(lane < (part + 1) * (rows // parts), occ[zb, part, xb], value)
    return value.astype(jnp.float32) * scale


def faces_kernel(density, znear, zfar, xnear, xfar, planes_got, blocks_got, tiles, sems):
    planes, columns, rows = density.shape
    wanted = [
        (density.at[0], planes_got.at[0]),
        (density.at[planes - 1], planes_got.at[1]),
        (density.at[:, pl.ds(0, BX), :], blocks_got.at[0]),
        (density.at[:, pl.ds(columns - BX, BX), :], blocks_got.at[1]),
    ]
    copies = [pltpu.make_async_copy(a, b, sems.at[i]) for i, (a, b) in enumerate(wanted)]
    for copy in copies:
        copy.start()
    for copy in copies:
        copy.wait()

    def face(side, row):
        tiles[...] = blocks_got[side].astype(jnp.float32).reshape(planes * BX, rows)
        return tiles[pl.ds(row, planes, stride=BX), :]

    zpair = planes_got[0].astype(jnp.float32), planes_got[1].astype(jnp.float32)
    xpair = face(0, 0), face(1, BX - 1)
    for axis, (low, high), near, far in (
        ("depth", zpair, znear, zfar), ("cols", xpair, xnear, xfar)
    ):
        odd = lax.rem(lax.axis_index(axis), 2) == 1
        near[...] = jnp.where(odd, low, high).astype(near.dtype)
        far[...] = jnp.where(odd, high, low).astype(far.dtype)


def faces(density):
    planes, columns, rows = density.shape
    vmem = pl.BlockSpec(memory_space=pltpu.VMEM)
    shapes = [(columns, rows)] * 2 + [(planes, rows)] * 2
    return pl.pallas_call(
        faces_kernel,
        in_specs=[pl.BlockSpec(memory_space=pltpu.HBM)],
        out_specs=[vmem] * 4,
        out_shape=[jax.ShapeDtypeStruct(shape, density.dtype) for shape in shapes],
        scratch_shapes=[
            pltpu.VMEM((2, columns, rows), density.dtype),
            pltpu.VMEM((2, planes, BX, rows), density.dtype),
            pltpu.VMEM((planes * BX, rows), jnp.float32),
            pltpu.SemaphoreType.DMA((4,)),
        ],
        compiler_params=pltpu.CompilerParams(vmem_limit_bytes=FACES_LIMIT),
    )(density)


def prepare_kernel(density, field, slope, diff):
    planes, columns, rows = density.shape
    diff[...] = difference_matrix(rows)

    @pl.loop(0, planes // 16)
    def _(k):
        at = pl.ds(16 * k, 16)
        part = density[at]
        field[at, 8:8 + columns, :] = part.astype(jnp.float32)
        step = jnp.dot(part.reshape(16 * columns, rows), diff[...],
                       preferred_element_type=jnp.float32)
        slope[at] = step.reshape(16, columns, rows)


def prepare(density):
    planes, columns, rows = density.shape
    vmem = pl.BlockSpec(memory_space=pltpu.VMEM)
    return pl.pallas_call(
        prepare_kernel,
        in_specs=[vmem],
        out_specs=[vmem] * 2,
        out_shape=[
            jax.ShapeDtypeStruct((planes, columns + 16, rows), jnp.float32),
            jax.ShapeDtypeStruct(density.shape, jnp.float32),
        ],
        scratch_shapes=[pltpu.VMEM((rows, rows), jnp.bfloat16)],
        cost_estimate=pl.CostEstimate(
            flops=2 * density.size * rows, bytes_accessed=10 * density.size, transcendentals=0
        ),
        compiler_params=pltpu.CompilerParams(vmem_limit_bytes=PREPARE_LIMIT),
    )(density)


def render_kernel(depth_scale, light_dir, pal, occ, field, slope, zlow, zhigh, xlow, xhigh,
                  out, edge, image):
    planes, columns, rows = slope.shape
    group = planes // occ.shape[0]
    f32 = jnp.float32
    edge[0] = xlow[...].astype(f32)
    edge[1] = xhigh[...].astype(f32)
    sublane = lax.broadcasted_iota(jnp.int32, (BX, rows), 0)
    light = [light_dir[i] for i in range(3)]
    half = [(0.5 * pal[0, c], 0.5 * pal[1, c]) for c in range(3)]
    extinct = (pal[0, 3] * LOG2E, pal[1, 3] * LOG2E)
    span = 2 * group
    steps = planes // span

    def march(block, outer):
        first = pl.multiple_of(block * BX, BX)
        lowest = (sublane == 0) & (block == 0)
        highest = (sublane == BX - 1) & (block != 0)

        def body(k, carry):
            total, through, red, green, blue, white = carry
            base = (steps - 1 - k) * span
            for zi in range(span - 1, -1, -1):
                if (zi + 1) % group == 0:
                    zb = base // group + zi // group
                    scale = occupied_row(occ, zb, block, rows, depth_scale)
                z = base + zi
                v = field[z, pl.ds(first + 8, BX), :]
                if zi == span - 1:
                    ahead = field[jnp.minimum(z + 1, planes - 1), pl.ds(first + 8, BX), :]
                    ahead = jnp.where(k == 0, zhigh[pl.ds(first, BX), :].astype(f32), ahead)
                else:
                    ahead = field[z + 1, pl.ds(first + 8, BX), :]
                if zi == 0:
                    behind = field[jnp.maximum(z - 1, 0), pl.ds(first + 8, BX), :]
                    ghost = zlow[pl.ds(first, BX), :].astype(f32)
                    behind = jnp.where(k == steps - 1, ghost, behind)
                else:
                    behind = field[z - 1, pl.ds(first + 8, BX), :]
                right = field[z, pl.ds(first + 9, BX), :]
                left = field[z, pl.ds(first + 7, BX), :]
                if outer:
                    right = jnp.where(highest, edge[1, pl.ds(z, 1), :], right)
                    left = jnp.where(lowest, edge[0, pl.ds(z, 1), :], left)
                gz = ahead - behind
                gx = right - left
                gy = slope[z, pl.ds(first, BX), :]
                norm = lax.rsqrt((gz * gz + gx * gx) + (gy * gy + 4.0))
                facing = (gz * light[0] + gx * light[1]) + gy * light[2]
                shade = jnp.abs(jnp.tanh(facing * norm)) + 3.0 / 7.0
                optical = jnp.log2(1.0 + jnp.exp2(v * extinct[0] + extinct[1]))
                total = total + scale * optical
                beyond = jnp.exp2(total)
                weight = (through - beyond) * shade
                through = beyond
                red = red + weight * jnp.tanh(v * half[0][0] + half[0][1])
                green = green + weight * jnp.tanh(v * half[1][0] + half[1][1])
                blue = blue + weight * jnp.tanh(v * half[2][0] + half[2][1])
                white = white + weight
            return total, through, red, green, blue, white

        zero = jnp.zeros((BX, rows), f32)
        total, _, red, green, blue, white = lax.fori_loop(
            0, steps, body, (zero, zero + 1.0, zero, zero, zero, zero)
        )
        at = pl.ds(first, BX)
        image[0, at, :] = 0.35 * (white + red)
        image[1, at, :] = 0.35 * (white + green)
        image[2, at, :] = 0.35 * (white + blue)
        image[3, at, :] = total

    last = columns // BX - 1

    @pl.loop(0, 2)
    def _(side):
        march(side * last, True)

    @pl.loop(1, last)
    def _(block):
        march(block, False)

    slabs, _, share, _ = out.shape
    for c in range(4):
        turned = encode((image[c] if c < 3 else -0.125 * image[c]).T)
        for d in range(slabs):
            out[d, c] = turned[d * share:(d + 1) * share, :]


def render(prepared, occ, light_dir, pal, halos, depth_scale, slabs):
    field, slope = prepared
    planes, columns, rows = slope.shape
    smem = pl.BlockSpec(memory_space=pltpu.SMEM)
    vmem = pl.BlockSpec(memory_space=pltpu.VMEM)
    return pl.pallas_call(
        lambda *refs: render_kernel(depth_scale, *refs),
        in_specs=[smem] * 3 + [vmem] * 6,
        out_specs=vmem,
        out_shape=jax.ShapeDtypeStruct((slabs, 4, rows // slabs, columns), jnp.int16),
        scratch_shapes=[
            pltpu.VMEM((2, planes, rows), jnp.float32),
            pltpu.VMEM((4, columns, rows), jnp.float32),
        ],
        compiler_params=pltpu.CompilerParams(vmem_limit_bytes=RENDER_LIMIT),
    )(light_dir, pal, occ, field, slope, *halos)


def composite(parts):
    slabs = parts.shape[0]
    parts = decode(parts)
    colours, total = parts[slabs - 1, :3], parts[slabs - 1, 3:]
    for d in range(slabs - 2, -1, -1):
        colours = colours + jnp.exp2(-8.0 * total) * parts[d, :3]
        total = total + parts[d, 3:]
    return jnp.concatenate([colours, 1.0 - jnp.exp2(-8.0 * total)], axis=0)


def encode(pixels):
    level = jnp.log2(jnp.maximum(pixels, 2.0 ** -24))
    code = (level * CODE_STEP + (CODE_TOP + 0.5)).astype(jnp.int32) - 32768
    return code.astype(jnp.int16)


def decode(codes):
    code = codes.astype(jnp.float32)
    level = code * (1.0 / CODE_STEP) + (32768.0 - CODE_TOP) / CODE_STEP
    return jnp.where(code > -32768.0, jnp.exp2(level), 0.0)


def neighbours(axis, near, far):
    size = lax.axis_size(axis)
    odd = lax.axis_index(axis) % 2 == 1
    evens = [pair for i in range(0, size - 1, 2) for pair in ((i, i + 1), (i + 1, i))]
    odds = [pair for i in range(1, size - 1, 2) for pair in ((i, i + 1), (i + 1, i))]
    from_far = lax.ppermute(far, axis, odds)
    from_near = lax.ppermute(near, axis, evens)
    return jnp.where(odd, from_near, from_far), jnp.where(odd, from_far, from_near)


def local(density, occupancy, light_dir, palette):
    planes, columns, rows = density.shape
    slabs = lax.axis_size("depth")
    devices = lax.axis_size("cols")
    znear, zfar, xnear, xfar = faces(density)
    zhalo = neighbours("depth", znear, zfar)
    xhalo = neighbours("cols", xnear, xfar)
    occ = occupancy.transpose(0, 2, 1)
    depth_scale = -3.0 / (planes * slabs)
    parts = render(prepare(density), occ, light_dir, palette.T, zhalo + xhalo, depth_scale, slabs)
    parts = lax.all_to_all(parts, "depth", 0, 0, tiled=True)
    codes = encode(composite(parts))
    codes = jnp.broadcast_to(codes[None], (devices,) + codes.shape)
    codes = lax.all_to_all(codes, "cols", 0, 0, tiled=True)
    return decode(codes).transpose(1, 0, 3, 2).reshape(4, devices * columns, rows // slabs)


def solution(mesh):
    placed = (P("depth", "cols", None), P("depth", "cols", None), P(), P())
    return jax.shard_map(
        local, mesh=mesh, in_specs=placed, out_specs=P(None, None, "depth"), check_vma=False
    )
```

```python
import jax
import jax.numpy as jnp
from jax import lax
from jax.experimental import pallas as pl
from jax.experimental.pallas import tpu as pltpu
from jax.sharding import PartitionSpec as P

BX = 16
LOG2E = 1.4426950408889634
CODE_TOP = 65535.0
CODE_STEP = CODE_TOP / 24.0
FACES_LIMIT = 53 * 1024 * 1024
PREPARE_LIMIT = 24 * 1024 * 1024
RENDER_LIMIT = 24 * 1024 * 1024


def difference_matrix(rows):
    row = lax.broadcasted_iota(jnp.int32, (rows, rows), 0)
    col = lax.broadcasted_iota(jnp.int32, (rows, rows), 1)
    ahead = (row == col + 1).astype(jnp.float32)
    behind = (row + 1 == col).astype(jnp.float32)
    return (ahead - behind).astype(jnp.bfloat16)


def occupied_row(occ, zb, xb, rows, scale):
    parts = occ.shape[1]
    lane = lax.broadcasted_iota(jnp.int32, (BX, rows), 1)
    value = jnp.broadcast_to(occ[zb, parts - 1, xb], (BX, rows))
    for part in range(parts - 2, -1, -1):
        value = jnp.where(lane < (part + 1) * (rows // parts), occ[zb, part, xb], value)
    return value.astype(jnp.float32) * scale


def faces_kernel(density, znear, zfar, xnear, xfar, planes_got, blocks_got, tiles, sems):
    planes, columns, rows = density.shape
    wanted = [
        (density.at[0], planes_got.at[0]),
        (density.at[planes - 1], planes_got.at[1]),
        (density.at[:, pl.ds(0, BX), :], blocks_got.at[0]),
        (density.at[:, pl.ds(columns - BX, BX), :], blocks_got.at[1]),
    ]
    copies = [pltpu.make_async_copy(a, b, sems.at[i]) for i, (a, b) in enumerate(wanted)]
    for copy in copies:
        copy.start()
    for copy in copies:
        copy.wait()

    def face(side, row):
        tiles[...] = blocks_got[side].astype(jnp.float32).reshape(planes * BX, rows)
        return tiles[pl.ds(row, planes, stride=BX), :]

    zpair = planes_got[0].astype(jnp.float32), planes_got[1].astype(jnp.float32)
    xpair = face(0, 0), face(1, BX - 1)
    for axis, (low, high), near, far in (
        ("depth", zpair, znear, zfar), ("cols", xpair, xnear, xfar)
    ):
        odd = lax.rem(lax.axis_index(axis), 2) == 1
        near[...] = jnp.where(odd, low, high).astype(near.dtype)
        far[...] = jnp.where(odd, high, low).astype(far.dtype)


def faces(density):
    planes, columns, rows = density.shape
    vmem = pl.BlockSpec(memory_space=pltpu.VMEM)
    shapes = [(columns, rows)] * 2 + [(planes, rows)] * 2
    return pl.pallas_call(
        faces_kernel,
        in_specs=[pl.BlockSpec(memory_space=pltpu.HBM)],
        out_specs=[vmem] * 4,
        out_shape=[jax.ShapeDtypeStruct(shape, density.dtype) for shape in shapes],
        scratch_shapes=[
            pltpu.VMEM((2, columns, rows), density.dtype),
            pltpu.VMEM((2, planes, BX, rows), density.dtype),
            pltpu.VMEM((planes * BX, rows), jnp.float32),
            pltpu.SemaphoreType.DMA((4,)),
        ],
        compiler_params=pltpu.CompilerParams(vmem_limit_bytes=FACES_LIMIT),
    )(density)


def prepare_kernel(density, field, slope, diff):
    planes, columns, rows = density.shape
    diff[...] = difference_matrix(rows)

    @pl.loop(0, planes // 64)
    def _(k):
        at = pl.ds(64 * k, 64)
        part = density[at]
        field[at, 8:8 + columns, :] = part.astype(jnp.float32)
        step = jnp.dot(part.reshape(64 * columns, rows), diff[...],
                       preferred_element_type=jnp.float32)
        slope[at] = step.reshape(64, columns, rows)


def prepare(density):
    planes, columns, rows = density.shape
    vmem = pl.BlockSpec(memory_space=pltpu.VMEM)
    return pl.pallas_call(
        prepare_kernel,
        in_specs=[vmem],
        out_specs=[vmem] * 2,
        out_shape=[
            jax.ShapeDtypeStruct((planes, columns + 16, rows), jnp.float32),
            jax.ShapeDtypeStruct(density.shape, jnp.float32),
        ],
        scratch_shapes=[pltpu.VMEM((rows, rows), jnp.bfloat16)],
        cost_estimate=pl.CostEstimate(
            flops=2 * density.size * rows, bytes_accessed=10 * density.size, transcendentals=0
        ),
        compiler_params=pltpu.CompilerParams(vmem_limit_bytes=PREPARE_LIMIT),
    )(density)


def render_kernel(depth_scale, light_dir, pal, occ, field, slope, zlow, zhigh, xlow, xhigh,
                  out, edge, image):
    planes, columns, rows = slope.shape
    group = planes // occ.shape[0]
    f32 = jnp.float32
    edge[0] = xlow[...].astype(f32)
    edge[1] = xhigh[...].astype(f32)
    sublane = lax.broadcasted_iota(jnp.int32, (BX, rows), 0)
    light = [light_dir[i] for i in range(3)]
    half = [(0.5 * pal[0, c], 0.5 * pal[1, c]) for c in range(3)]
    extinct = (pal[0, 3] * LOG2E, pal[1, 3] * LOG2E)
    span = 2 * group
    steps = planes // span

    def march(block, outer):
        first = pl.multiple_of(block * BX, BX)
        lowest = (sublane == 0) & (block == 0)
        highest = (sublane == BX - 1) & (block != 0)

        def body(k, carry):
            total, through, red, green, blue, white = carry
            base = (steps - 1 - k) * span
            for zi in range(span - 1, -1, -1):
                if (zi + 1) % group == 0:
                    zb = base // group + zi // group
                    scale = occupied_row(occ, zb, block, rows, depth_scale)
                z = base + zi
                v = field[z, pl.ds(first + 8, BX), :]
                if zi == span - 1:
                    ahead = field[jnp.minimum(z + 1, planes - 1), pl.ds(first + 8, BX), :]
                    ahead = jnp.where(k == 0, zhigh[pl.ds(first, BX), :].astype(f32), ahead)
                else:
                    ahead = field[z + 1, pl.ds(first + 8, BX), :]
                if zi == 0:
                    behind = field[jnp.maximum(z - 1, 0), pl.ds(first + 8, BX), :]
                    ghost = zlow[pl.ds(first, BX), :].astype(f32)
                    behind = jnp.where(k == steps - 1, ghost, behind)
                else:
                    behind = field[z - 1, pl.ds(first + 8, BX), :]
                right = field[z, pl.ds(first + 9, BX), :]
                left = field[z, pl.ds(first + 7, BX), :]
                if outer:
                    right = jnp.where(highest, edge[1, pl.ds(z, 1), :], right)
                    left = jnp.where(lowest, edge[0, pl.ds(z, 1), :], left)
                gz = ahead - behind
                gx = right - left
                gy = slope[z, pl.ds(first, BX), :]
                norm = lax.rsqrt((gz * gz + gx * gx) + (gy * gy + 4.0))
                facing = (gz * light[0] + gx * light[1]) + gy * light[2]
                shade = jnp.abs(jnp.tanh(facing * norm)) + 3.0 / 7.0
                optical = jnp.log2(1.0 + jnp.exp2(v * extinct[0] + extinct[1]))
                total = total + scale * optical
                beyond = jnp.exp2(total)
                weight = (through - beyond) * shade
                through = beyond
                red = red + weight * jnp.tanh(v * half[0][0] + half[0][1])
                green = green + weight * jnp.tanh(v * half[1][0] + half[1][1])
                blue = blue + weight * jnp.tanh(v * half[2][0] + half[2][1])
                white = white + weight
            return total, through, red, green, blue, white

        zero = jnp.zeros((BX, rows), f32)
        total, _, red, green, blue, white = lax.fori_loop(
            0, steps, body, (zero, zero + 1.0, zero, zero, zero, zero)
        )
        at = pl.ds(first, BX)
        image[0, at, :] = 0.35 * (white + red)
        image[1, at, :] = 0.35 * (white + green)
        image[2, at, :] = 0.35 * (white + blue)
        image[3, at, :] = total

    last = columns // BX - 1

    @pl.loop(0, 2)
    def _(side):
        march(side * last, True)

    @pl.loop(1, last)
    def _(block):
        march(block, False)

    slabs, _, share, _ = out.shape
    for c in range(4):
        turned = encode((image[c] if c < 3 else -0.125 * image[c]).T)
        for d in range(slabs):
            out[d, c] = turned[d * share:(d + 1) * share, :]


def render(prepared, occ, light_dir, pal, halos, depth_scale, slabs):
    field, slope = prepared
    planes, columns, rows = slope.shape
    smem = pl.BlockSpec(memory_space=pltpu.SMEM)
    vmem = pl.BlockSpec(memory_space=pltpu.VMEM)
    return pl.pallas_call(
        lambda *refs: render_kernel(depth_scale, *refs),
        in_specs=[smem] * 3 + [vmem] * 6,
        out_specs=vmem,
        out_shape=jax.ShapeDtypeStruct((slabs, 4, rows // slabs, columns), jnp.int16),
        scratch_shapes=[
            pltpu.VMEM((2, planes, rows), jnp.float32),
            pltpu.VMEM((4, columns, rows), jnp.float32),
        ],
        compiler_params=pltpu.CompilerParams(vmem_limit_bytes=RENDER_LIMIT),
    )(light_dir, pal, occ, field, slope, *halos)


def composite(parts):
    slabs = parts.shape[0]
    parts = decode(parts)
    colours, total = parts[slabs - 1, :3], parts[slabs - 1, 3:]
    for d in range(slabs - 2, -1, -1):
        colours = colours + jnp.exp2(-8.0 * total) * parts[d, :3]
        total = total + parts[d, 3:]
    return jnp.concatenate([colours, 1.0 - jnp.exp2(-8.0 * total)], axis=0)


def encode(pixels):
    level = jnp.log2(jnp.maximum(pixels, 2.0 ** -24))
    code = (level * CODE_STEP + (CODE_TOP + 0.5)).astype(jnp.int32) - 32768
    return code.astype(jnp.int16)


def decode(codes):
    code = codes.astype(jnp.float32)
    level = code * (1.0 / CODE_STEP) + (32768.0 - CODE_TOP) / CODE_STEP
    return jnp.where(code > -32768.0, jnp.exp2(level), 0.0)


def neighbours(axis, near, far):
    size = lax.axis_size(axis)
    odd = lax.axis_index(axis) % 2 == 1
    evens = [pair for i in range(0, size - 1, 2) for pair in ((i, i + 1), (i + 1, i))]
    odds = [pair for i in range(1, size - 1, 2) for pair in ((i, i + 1), (i + 1, i))]
    from_far = lax.ppermute(far, axis, odds)
    from_near = lax.ppermute(near, axis, evens)
    return jnp.where(odd, from_near, from_far), jnp.where(odd, from_far, from_near)


def local(density, occupancy, light_dir, palette):
    planes, columns, rows = density.shape
    slabs = lax.axis_size("depth")
    devices = lax.axis_size("cols")
    znear, zfar, xnear, xfar = faces(density)
    zhalo = neighbours("depth", znear, zfar)
    xhalo = neighbours("cols", xnear, xfar)
    occ = occupancy.transpose(0, 2, 1)
    depth_scale = -3.0 / (planes * slabs)
    parts = render(prepare(density), occ, light_dir, palette.T, zhalo + xhalo, depth_scale, slabs)
    parts = lax.all_to_all(parts, "depth", 0, 0, tiled=True)
    codes = encode(composite(parts))
    codes = jnp.broadcast_to(codes[None], (devices,) + codes.shape)
    codes = lax.all_to_all(codes, "cols", 0, 0, tiled=True)
    return decode(codes).transpose(1, 0, 3, 2).reshape(4, devices * columns, rows // slabs)


def solution(mesh):
    placed = (P("depth", "cols", None), P("depth", "cols", None), P(), P())
    return jax.shard_map(
        local, mesh=mesh, in_specs=placed, out_specs=P(None, None, "depth"), check_vma=False
    )
```

```python
import jax
import jax.numpy as jnp
from jax import lax
from jax.experimental import pallas as pl
from jax.experimental.pallas import tpu as pltpu
from jax.sharding import PartitionSpec as P

BX = 16
LOG2E = 1.4426950408889634
CODE_TOP = 65535.0
CODE_STEP = CODE_TOP / 24.0
FACES_LIMIT = 53 * 1024 * 1024
PREPARE_LIMIT = 24 * 1024 * 1024
RENDER_LIMIT = 24 * 1024 * 1024


def difference_matrix(rows):
    row = lax.broadcasted_iota(jnp.int32, (rows, rows), 0)
    col = lax.broadcasted_iota(jnp.int32, (rows, rows), 1)
    ahead = (row == col + 1).astype(jnp.float32)
    behind = (row + 1 == col).astype(jnp.float32)
    return (ahead - behind).astype(jnp.bfloat16)


def occupied_row(occ, zb, xb, rows, scale):
    parts = occ.shape[1]
    lane = lax.broadcasted_iota(jnp.int32, (BX, rows), 1)
    value = jnp.broadcast_to(occ[zb, parts - 1, xb], (BX, rows))
    for part in range(parts - 2, -1, -1):
        value = jnp.where(lane < (part + 1) * (rows // parts), occ[zb, part, xb], value)
    return value.astype(jnp.float32) * scale


def faces_kernel(density, znear, zfar, xnear, xfar, planes_got, blocks_got, tiles, sems):
    planes, columns, rows = density.shape
    wanted = [
        (density.at[0], planes_got.at[0]),
        (density.at[planes - 1], planes_got.at[1]),
        (density.at[:, pl.ds(0, BX), :], blocks_got.at[0]),
        (density.at[:, pl.ds(columns - BX, BX), :], blocks_got.at[1]),
    ]
    copies = [pltpu.make_async_copy(a, b, sems.at[i]) for i, (a, b) in enumerate(wanted)]
    for copy in copies:
        copy.start()
    for copy in copies:
        copy.wait()

    def face(side, row):
        block = blocks_got[side].astype(jnp.float32)
        tiles[0:planes * BX, :] = block.reshape(planes * BX, rows)
        return tiles[pl.ds(row, planes, stride=BX), :]

    zpair = planes_got[0].astype(jnp.float32), planes_got[1].astype(jnp.float32)
    xpair = face(0, 0), face(1, BX - 1)
    for axis, (low, high), near, far in (
        ("depth", zpair, znear, zfar), ("cols", xpair, xnear, xfar)
    ):
        odd = lax.rem(lax.axis_index(axis), 2) == 1
        near[...] = jnp.where(odd, low, high).astype(near.dtype)
        far[...] = jnp.where(odd, high, low).astype(far.dtype)


def faces(density):
    planes, columns, rows = density.shape
    vmem = pl.BlockSpec(memory_space=pltpu.VMEM)
    shapes = [(columns, rows)] * 2 + [(planes, rows)] * 2
    return pl.pallas_call(
        faces_kernel,
        in_specs=[pl.BlockSpec(memory_space=pltpu.HBM)],
        out_specs=[vmem] * 4,
        out_shape=[jax.ShapeDtypeStruct(shape, density.dtype) for shape in shapes],
        scratch_shapes=[
            pltpu.VMEM((2, columns, rows), density.dtype),
            pltpu.VMEM((2, planes, BX, rows), density.dtype),
            pltpu.VMEM(((planes + 1) * BX, rows), jnp.float32),
            pltpu.SemaphoreType.DMA((4,)),
        ],
        compiler_params=pltpu.CompilerParams(vmem_limit_bytes=FACES_LIMIT),
    )(density)


def prepare_kernel(density, field, slope, diff):
    planes, columns, rows = density.shape
    diff[...] = difference_matrix(rows)

    @pl.loop(0, planes // 64)
    def _(k):
        at = pl.ds(64 * k, 64)
        part = density[at]
        field[at, 8:8 + columns, :] = part.astype(jnp.float32)
        step = jnp.dot(part.reshape(64 * columns, rows), diff[...],
                       preferred_element_type=jnp.float32)
        slope[at] = step.reshape(64, columns, rows)


def prepare(density):
    planes, columns, rows = density.shape
    vmem = pl.BlockSpec(memory_space=pltpu.VMEM)
    return pl.pallas_call(
        prepare_kernel,
        in_specs=[vmem],
        out_specs=[vmem] * 2,
        out_shape=[
            jax.ShapeDtypeStruct((planes, columns + 16, rows), jnp.float32),
            jax.ShapeDtypeStruct(density.shape, jnp.float32),
        ],
        scratch_shapes=[pltpu.VMEM((rows, rows), jnp.bfloat16)],
        cost_estimate=pl.CostEstimate(
            flops=2 * density.size * rows, bytes_accessed=10 * density.size, transcendentals=0
        ),
        compiler_params=pltpu.CompilerParams(vmem_limit_bytes=PREPARE_LIMIT),
    )(density)


def render_kernel(depth_scale, light_dir, pal, occ, field, slope, zlow, zhigh, xlow, xhigh,
                  out, edge, image):
    planes, columns, rows = slope.shape
    group = planes // occ.shape[0]
    f32 = jnp.float32
    edge[0] = xlow[...].astype(f32)
    edge[1] = xhigh[...].astype(f32)
    sublane = lax.broadcasted_iota(jnp.int32, (BX, rows), 0)
    light = [light_dir[i] for i in range(3)]
    half = [(0.5 * pal[0, c], 0.5 * pal[1, c]) for c in range(3)]
    extinct = (pal[0, 3] * LOG2E, pal[1, 3] * LOG2E)
    span = 2 * group
    steps = planes // span

    def march(block, outer):
        first = pl.multiple_of(block * BX, BX)
        lowest = (sublane == 0) & (block == 0)
        highest = (sublane == BX - 1) & (block != 0)

        def body(k, carry):
            total, through, red, green, blue, white = carry
            base = (steps - 1 - k) * span
            for zi in range(span - 1, -1, -1):
                if (zi + 1) % group == 0:
                    zb = base // group + zi // group
                    scale = occupied_row(occ, zb, block, rows, depth_scale)
                z = base + zi
                v = field[z, pl.ds(first + 8, BX), :]
                if zi == span - 1:
                    ahead = field[jnp.minimum(z + 1, planes - 1), pl.ds(first + 8, BX), :]
                    ahead = jnp.where(k == 0, zhigh[pl.ds(first, BX), :].astype(f32), ahead)
                else:
                    ahead = field[z + 1, pl.ds(first + 8, BX), :]
                if zi == 0:
                    behind = field[jnp.maximum(z - 1, 0), pl.ds(first + 8, BX), :]
                    ghost = zlow[pl.ds(first, BX), :].astype(f32)
                    behind = jnp.where(k == steps - 1, ghost, behind)
                else:
                    behind = field[z - 1, pl.ds(first + 8, BX), :]
                right = field[z, pl.ds(first + 9, BX), :]
                left = field[z, pl.ds(first + 7, BX), :]
                if outer:
                    right = jnp.where(highest, edge[1, pl.ds(z, 1), :], right)
                    left = jnp.where(lowest, edge[0, pl.ds(z, 1), :], left)
                gz = ahead - behind
                gx = right - left
                gy = slope[z, pl.ds(first, BX), :]
                norm = lax.rsqrt((gz * gz + gx * gx) + (gy * gy + 4.0))
                facing = (gz * light[0] + gx * light[1]) + gy * light[2]
                shade = jnp.abs(jnp.tanh(facing * norm)) + 3.0 / 7.0
                optical = jnp.log2(1.0 + jnp.exp2(v * extinct[0] + extinct[1]))
                total = total + scale * optical
                beyond = jnp.exp2(total)
                weight = (through - beyond) * shade
                through = beyond
                red = red + weight * jnp.tanh(v * half[0][0] + half[0][1])
                green = green + weight * jnp.tanh(v * half[1][0] + half[1][1])
                blue = blue + weight * jnp.tanh(v * half[2][0] + half[2][1])
                white = white + weight
            return total, through, red, green, blue, white

        zero = jnp.zeros((BX, rows), f32)
        total, _, red, green, blue, white = lax.fori_loop(
            0, steps, body, (zero, zero + 1.0, zero, zero, zero, zero)
        )
        at = pl.ds(first, BX)
        image[0, at, :] = 0.35 * (white + red)
        image[1, at, :] = 0.35 * (white + green)
        image[2, at, :] = 0.35 * (white + blue)
        image[3, at, :] = total

    last = columns // BX - 1

    @pl.loop(0, 2)
    def _(side):
        march(side * last, True)

    @pl.loop(1, last)
    def _(block):
        march(block, False)

    slabs, _, share, _ = out.shape
    for c in range(4):
        turned = encode((image[c] if c < 3 else -0.125 * image[c]).T)
        for d in range(slabs):
            out[d, c] = turned[d * share:(d + 1) * share, :]


def render(prepared, occ, light_dir, pal, halos, depth_scale, slabs):
    field, slope = prepared
    planes, columns, rows = slope.shape
    smem = pl.BlockSpec(memory_space=pltpu.SMEM)
    vmem = pl.BlockSpec(memory_space=pltpu.VMEM)
    return pl.pallas_call(
        lambda *refs: render_kernel(depth_scale, *refs),
        in_specs=[smem] * 3 + [vmem] * 6,
        out_specs=vmem,
        out_shape=jax.ShapeDtypeStruct((slabs, 4, rows // slabs, columns), jnp.int16),
        scratch_shapes=[
            pltpu.VMEM((2, planes, rows), jnp.float32),
            pltpu.VMEM((4, columns, rows), jnp.float32),
        ],
        compiler_params=pltpu.CompilerParams(vmem_limit_bytes=RENDER_LIMIT),
    )(light_dir, pal, occ, field, slope, *halos)


def composite(parts):
    slabs = parts.shape[0]
    parts = decode(parts)
    colours, total = parts[slabs - 1, :3], parts[slabs - 1, 3:]
    for d in range(slabs - 2, -1, -1):
        colours = colours + jnp.exp2(-8.0 * total) * parts[d, :3]
        total = total + parts[d, 3:]
    return jnp.concatenate([colours, 1.0 - jnp.exp2(-8.0 * total)], axis=0)


def encode(pixels):
    level = jnp.log2(jnp.maximum(pixels, 2.0 ** -24))
    code = (level * CODE_STEP + (CODE_TOP + 0.5)).astype(jnp.int32) - 32768
    return code.astype(jnp.int16)


def decode(codes):
    code = codes.astype(jnp.float32)
    level = code * (1.0 / CODE_STEP) + (32768.0 - CODE_TOP) / CODE_STEP
    return jnp.where(code > -32768.0, jnp.exp2(level), 0.0)


def neighbours(axis, near, far):
    size = lax.axis_size(axis)
    odd = lax.axis_index(axis) % 2 == 1
    evens = [pair for i in range(0, size - 1, 2) for pair in ((i, i + 1), (i + 1, i))]
    odds = [pair for i in range(1, size - 1, 2) for pair in ((i, i + 1), (i + 1, i))]
    from_far = lax.ppermute(far, axis, odds)
    from_near = lax.ppermute(near, axis, evens)
    return jnp.where(odd, from_near, from_far), jnp.where(odd, from_far, from_near)


def local(density, occupancy, light_dir, palette):
    planes, columns, rows = density.shape
    slabs = lax.axis_size("depth")
    devices = lax.axis_size("cols")
    znear, zfar, xnear, xfar = faces(density)
    zhalo = neighbours("depth", znear, zfar)
    xhalo = neighbours("cols", xnear, xfar)
    occ = occupancy.transpose(0, 2, 1)
    depth_scale = -3.0 / (planes * slabs)
    parts = render(prepare(density), occ, light_dir, palette.T, zhalo + xhalo, depth_scale, slabs)
    parts = lax.all_to_all(parts, "depth", 0, 0, tiled=True)
    codes = encode(composite(parts))
    codes = jnp.broadcast_to(codes[None], (devices,) + codes.shape)
    codes = lax.all_to_all(codes, "cols", 0, 0, tiled=True)
    return decode(codes).transpose(1, 0, 3, 2).reshape(4, devices * columns, rows // slabs)


def solution(mesh):
    placed = (P("depth", "cols", None), P("depth", "cols", None), P(), P())
    return jax.shard_map(
        local, mesh=mesh, in_specs=placed, out_specs=P(None, None, "depth"), check_vma=False
    )
```
